32 devices in a mesh: group: 2 (over y), expert: 4 (over x, core), replica: 4 (over z).
Axes of the slice: x: 2, y: 2, z: 4, core: 2. Of those that a mesh axis runs over, the one named last changes fastest.
Arguments:
- tokens: bfloat16 [1024, 7168], P(('group', 'expert')), parts along dimension 0, may hold values from -6 to 6
- route_ids: int32 [1024, 8], P(('group', 'expert')), parts along dimension 0, may hold values from 0 to 255, all different within a row
- route_gates: float32 [1024, 8], P(('group', 'expert')), parts along dimension 0, may hold values from 0.2 to 1
- copy_source: int32 [8], P('group'), parts along dimension 0, may hold values from 0 to 3, each once
- copy_share: int32 [8], P('group'), parts along dimension 0, may hold values from 0 to 128, as said below
- w_gate_up: bfloat16 [4, 7168, 2, 1024], P('expert', None, None, 'replica'), may hold values from -0.0625 to 0.0625
- w_down: bfloat16 [4, 1024, 7168], P('expert', 'replica'), may hold values from -0.1875 to 0.1875
- shared_gate_up: bfloat16 [7168, 2, 1024], P(None, None, 'replica'), may hold values from -0.0625 to 0.0625
- shared_down: bfloat16 [1024, 7168], P('replica'), may hold values from -0.1875 to 0.1875
Outputs:
- mixed: bfloat16 [1024, 7168], P(('group', 'expert', 'replica')), parts along dimension 0
The draws below stay inside these ranges and needn't reach their ends.
There are 2 independent parts, one for each index of `group`. The reference program is written for one: setup_inputs(seed, part) draws one part's arguments, and reference() takes and returns one part's arrays. A program takes and returns all parts, laid end to end along the dimension named above; an argument that names none is the same for every part. Nothing has to cross between parts.
Inputs may be any that keep to these rules, and one draw needn't show every extreme that they name: `copy_source`: every expert of the layer appears exactly once. `copy_share`: some expert has 0 and another has 128. `route_ids`: the 8 experts of a token are distinct.
All inputs are finite; a program needn't handle non-finite values.
Results may differ from the reference program's by a relative error of at most 0.0051.
Values may be sent and summed in bfloat16 or wider, within the bound.
No kernel may reach another device: no remote copies, remote signals or barrier semaphores. Data moves between devices by JAX's collectives and lax.ppermute only.
A program may use at most 128 MiB of HBM per device.

```python
import jax
import jax.numpy as jnp
from jax import lax

D = 7168
EXPERTS_ALL = 256
TOP = 8
HID = 1024
SHID = 1024
TOK_ROW = 128
EXPERTS = 4
TOKENS = 512
CAP = 6
SLICE = 256


def draw_copy_share(key, part):
    key = jax.random.fold_in(key, 11)
    value_key, order_key = jax.random.split(key)
    values = jax.random.randint(value_key, (EXPERTS,), 0, TOK_ROW + 1)
    order = jax.random.permutation(order_key, EXPERTS)
    values = values.at[order[0]].set(0).at[order[1]].set(TOK_ROW)
    return values.astype(jnp.int32)


def levels(own_key, shape, cuts, least, high):
    loudness, own = 1.0, jax.random.fold_in(own_key, 6)
    for dim, parts in cuts:
        steps = jnp.exp(jax.random.uniform(jax.random.fold_in(own, dim), (parts,), jnp.float32, least / len(cuts), high / len(cuts)))
        loudness = loudness * jnp.repeat(steps, shape[dim] // parts).reshape([-1 if axis == dim else 1 for axis in range(len(shape))])
    return loudness


def picks_of(own_key, rows, amount, top, lift):
    sequence = jax.random.permutation(jax.random.fold_in(own_key, 1), amount)
    favour = sequence
    for power in range(3):
        favour = favour * favour // amount
    favour = favour * lift // amount
    tickets = jax.random.randint(jax.random.fold_in(own_key, 2), (rows, amount), 0, 4096) + favour
    sure = jax.random.permutation(jax.random.fold_in(own_key, 3), rows)[jnp.arange(amount) % rows]
    tickets = jnp.where(jnp.arange(rows)[:, None] == sure[None, :], 1 << 14, tickets)
    priority = tickets * amount + jnp.arange(amount)
    return lax.top_k(priority.astype(jnp.int32), top)[1].astype(jnp.int32)


def scatter_about(rng, dims, scale, limit, cuts=(), kind=jnp.bfloat16):
    entries = jax.random.normal(rng, dims, jnp.float32) * scale
    if len(cuts) > 0:
        entries = levels(rng, dims, cuts, -0.22, 0.18) * entries
    return jnp.clip(entries, min=-limit, max=limit).astype(kind)


def setup_inputs(seed: int = 0, part: int = 0) -> dict:
    streams_of = jax.random.split(jax.random.key(seed), 10)
    own_keys = jax.random.split(jax.random.fold_in(streams_of[9], part), 10)
    return {
        "tokens": scatter_about(own_keys[0], (TOKENS, D), 1.0, 6.0, ((0, 4),)),
        "route_ids": picks_of(own_keys[1], TOKENS, EXPERTS_ALL, TOP, 512),
        "route_gates": jnp.clip(0.2 + 0.8 * jax.random.uniform(own_keys[2], (TOKENS, TOP), jnp.float32) ** levels(own_keys[2], (TOKENS, TOP), ((0, 4),), -0.2, 0.2), 0.2, 1.0),
        "copy_source": jax.random.permutation(own_keys[3], EXPERTS).astype(jnp.int32),
        "copy_share": draw_copy_share(jax.random.fold_in(jax.random.fold_in(streams_of[9], part), 71), part),
        "w_gate_up": scatter_about(streams_of[5], (EXPERTS, D, 2, HID), D ** -0.5, 0.0625, ((0, 4), (3, 4))),
        "w_down": scatter_about(streams_of[6], (EXPERTS, HID, D), HID ** -0.5, 0.1875, ((0, 4), (1, 4))),
        "shared_gate_up": scatter_about(streams_of[7], (D, 2, SHID), D ** -0.5, 0.0625, ((2, 4),)),
        "shared_down": scatter_about(streams_of[8], (SHID, D), SHID ** -0.5, 0.1875, ((0, 4),)),
    }


def plan_block(route_rows, copy_source, copy_share, experts, capacity):
    row_count, top_count = route_rows.shape
    inside = route_rows < experts
    expert = jnp.where(inside, route_rows, 0).astype(jnp.int32)
    holders = jnp.arange(experts, dtype=jnp.int32)
    flattened = expert.reshape(-1)
    matches = flattened[:, None] == holders[None, :]
    share_limit = jnp.sum(jnp.where(matches, copy_share[None, :], 0), axis=1).astype(jnp.int32).reshape(row_count, top_count)
    new_home = jnp.sum(jnp.where(copy_source[None, :] == flattened[:, None], holders[None, :], 0), axis=1).astype(jnp.int32).reshape(row_count, top_count)
    position = jnp.arange(row_count, dtype=jnp.int32)[:, None]
    by_copy = inside & (position < share_limit)
    holder = jnp.where(by_copy, new_home, expert).astype(jnp.int32)
    member = ((holder.reshape(-1)[:, None] == holders[None, :]) & inside.reshape(-1)[:, None]).astype(jnp.int32)
    before = jnp.cumsum(member, axis=0) - member
    rank_index = jnp.sum(before * member, axis=1).astype(jnp.int32).reshape(row_count, top_count)
    served = inside & (rank_index < capacity)
    return expert, by_copy, holder, rank_index, served


def reference(tokens, route_ids, route_gates, copy_source, copy_share, w_gate_up, w_down, shared_gate_up, shared_down):
    blocks = route_ids.reshape(EXPERTS, TOK_ROW, TOP)
    expert, by_copy, holder, rank_index, served = jax.vmap(
        lambda part_rows: plan_block(part_rows, copy_source, copy_share, EXPERTS, CAP))(blocks)
    slot_count = 2 * CAP
    table_width = EXPERTS * slot_count
    dump_index = EXPERTS * table_width
    block_index = jnp.arange(EXPERTS, dtype=jnp.int32)[:, None, None]
    token_index = block_index * TOK_ROW + jnp.arange(TOK_ROW, dtype=jnp.int32)[None, :, None] + jnp.zeros((1, 1, TOP), jnp.int32)
    slot_index = rank_index + CAP * by_copy.astype(jnp.int32)
    position = jnp.where(served, expert * table_width + block_index * slot_count + slot_index, dump_index).reshape(-1).astype(jnp.int32)
    gate_values = jnp.where(served, route_gates.reshape(EXPERTS, TOK_ROW, TOP), 0.0).reshape(-1)
    token_table = jnp.zeros((dump_index + 1,), jnp.int32).at[position].set(token_index.reshape(-1))[:dump_index]
    gate_table = jnp.zeros((dump_index + 1,), jnp.float32).at[position].set(gate_values)[:dump_index]
    token_table = token_table.reshape(EXPERTS, table_width)
    gate_table = gate_table.reshape(EXPERTS, table_width)

    def one_expert(operands):
        row_ids, weights, up_weights, down_weights = operands
        input_rows = tokens[row_ids]
        projected = jnp.dot(input_rows, up_weights.reshape(D, 2 * HID), preferred_element_type=jnp.float32)
        hidden = (jax.nn.silu(projected[:, :HID]) * projected[:, HID:]).astype(jnp.bfloat16)
        slice_parts = jnp.einsum("rsh,shd->rsd",
                                 hidden.reshape(table_width, HID // SLICE, SLICE).astype(jnp.float32),
                                 down_weights.reshape(HID // SLICE, SLICE, D).astype(jnp.float32))
        rounded = lax.optimization_barrier(slice_parts.astype(jnp.bfloat16))
        return jnp.sum(rounded.astype(jnp.float32), axis=1) * weights[:, None]

    contrib = lax.map(one_expert, (token_table, gate_table, w_gate_up, w_down))
    routed = jax.ops.segment_sum(contrib.reshape(-1, D), token_table.reshape(-1), num_segments=TOKENS)
    shared_projected = jnp.dot(tokens, shared_gate_up.reshape(D, 2 * SHID), preferred_element_type=jnp.float32)
    shared_hidden = (jax.nn.silu(shared_projected[:, :SHID]) * shared_projected[:, SHID:]).astype(jnp.bfloat16)
    shared_out = jnp.dot(shared_hidden, shared_down, preferred_element_type=jnp.float32)
    return (shared_out + routed).astype(jnp.bfloat16)
```

```python
import functools

import jax
import jax.numpy as jnp
from jax import lax
from jax.experimental import pallas as pl
from jax.experimental.pallas import tpu as pltpu
from jax.sharding import PartitionSpec as P

BF16 = jnp.bfloat16
F32 = jnp.float32
I32 = jnp.int32
PIECE = 256
MIB = 1 << 20


def iota(shape, dim):
    return lax.broadcasted_iota(I32, shape, dim)


def dot(a, b):
    return jnp.dot(a, b, preferred_element_type=F32)


def in_hbm(*arrays):
    return [pltpu.with_memory_space_constraint(array, pltpu.HBM) for array in arrays]


def chunk_count(width):
    for count in (4, 2, 1):
        if width % (count * PIECE) == 0:
            return count
    raise ValueError(width)


def plan_kernel(experts, capacity, share_hbm, source_hbm, ids_hbm, gates_hbm, tokens_hbm, gate_out, tokens_ref, *rest):
    outs, (share_ref, source_ref, ids_ref, gates_ref, sems) = rest[:experts], rest[experts:]
    copies = [
        pltpu.make_async_copy(source, target, sems.at[number])
        for number, (source, target) in enumerate(
            [
                (ids_hbm, ids_ref),
                (share_hbm, share_ref),
                (source_hbm, source_ref),
                (gates_hbm, gates_ref),
                (tokens_hbm, tokens_ref),
            ]
        )
    ]
    for copy in copies:
        copy.start()
    for copy in copies[:-1]:
        copy.wait()
    ids = ids_ref[...]
    gates = gates_ref[...]
    top, rows = ids.shape
    me = lax.axis_index("expert")
    inside = ids < experts
    limit = jnp.zeros_like(ids)
    home = jnp.zeros_like(ids)
    for index in range(experts):
        limit = jnp.where(ids == index, share_ref[index], limit)
        home = jnp.where(ids == source_ref[index], index, home)
    by_copy = inside & (iota((top, rows), 1) < limit)
    holder = jnp.where(by_copy, home, ids)
    members = [jnp.where(inside & (holder == index), 1.0, 0.0) for index in range(experts)]
    earlier = jnp.where(iota((rows, rows), 0) < iota((rows, rows), 1), 1.0, 0.0).astype(BF16)
    rank = jnp.zeros((top, rows), F32)
    for index in range(experts):
        member = members[index]
        counts = jnp.broadcast_to(jnp.sum(member, axis=0, keepdims=True), (8, rows))
        running = dot(counts.astype(BF16), earlier)[:1]
        lines = []
        for k in range(top):
            lines.append(running)
            running = running + member[k : k + 1]
        rank = rank + member * jnp.concatenate(lines, axis=0)
    rank = rank.astype(I32)
    served = inside & (rank < capacity)
    slots = 2 * capacity
    place = jnp.where(served, ids * slots + rank + jnp.where(by_copy, capacity, 0), -1)
    seat = jnp.where(served, holder * capacity + rank, -1)
    seats = jnp.zeros((rows, rows), F32)
    for k in range(top):
        seats = seats + jnp.where(seat[k : k + 1] == iota((rows, rows), 0), gates[k : k + 1], 0.0)
    gate_out[...] = seats.T
    height = experts * 2 * slots
    line = iota((height, 1), 0)
    within = lax.rem(line, 2 * slots)
    wanted = (me ^ (line // (2 * slots))) * slots + lax.rem(within, slots)
    pick = jnp.zeros((height, rows), F32)
    for k in range(top):
        pick = pick + jnp.where(place[k : k + 1] == wanted, 1.0, 0.0)
    first = jnp.where(within < slots, pick, 0.0).astype(BF16)
    second = jnp.where(within < slots, 0.0, pick).astype(BF16)
    copies[-1].wait()
    half = tokens_ref.shape[1] // 2
    step = half // chunk_count(half) if half % PIECE == 0 else half
    for start in range(0, half, step):
        picked = dot(first, tokens_ref[:, start : start + step]) + dot(
            second, tokens_ref[:, half + start : half + start + step]
        )
        for index in range(experts):
            outs[index][:, start : start + step] = picked[
                index * 2 * slots : (index + 1) * 2 * slots
            ].astype(BF16)


def plan(route_ids, route_gates, copy_source, copy_share, tokens, experts, capacity):
    rows, width = tokens.shape
    vmem = pl.BlockSpec(memory_space=pltpu.VMEM)
    hbm = pl.BlockSpec(memory_space=pltpu.HBM)
    return pl.pallas_call(
        functools.partial(plan_kernel, experts, capacity),
        out_shape=[pltpu.VMEM((rows, rows), F32), pltpu.VMEM((rows, width), BF16)]
        + [pltpu.VMEM((4 * capacity, width // 2), BF16)] * experts,
        in_specs=[hbm] * 5,
        out_specs=[vmem] * (experts + 2),
        scratch_shapes=[
            pltpu.SMEM(copy_share.shape, I32),
            pltpu.SMEM(copy_source.shape, I32),
            pltpu.VMEM(route_ids.shape[::-1], I32),
            pltpu.VMEM(route_gates.shape[::-1], F32),
            pltpu.SemaphoreType.DMA((5,)),
        ],
        compiler_params=pltpu.CompilerParams(vmem_limit_bytes=16 * MIB),
        cost_estimate=pl.CostEstimate(flops=10**8, bytes_accessed=4 * 10**6, transcendentals=0),
        name="plan",
    )(*in_hbm(copy_share, copy_source, route_ids.T, route_gates.T, tokens))


def doubler():
    shape = (PIECE, 2 * PIECE)
    return jnp.where(iota(shape, 1) // 2 == iota(shape, 0), 1.0, 0.0).astype(BF16)


def spread(block, twice):
    parts = []
    for start in range(0, block.shape[1], PIECE):
        both = dot(block[:, start : start + PIECE], twice)
        even = lax.rem(iota(both.shape, 1), 2) == 0
        gate = jnp.where(even, both, 0.0).astype(BF16)
        up = jnp.where(even, 0.0, both).astype(BF16)
        parts.append(jnp.concatenate([gate, up], axis=0))
    return jnp.concatenate(parts, axis=1)


def gated(total):
    rows = total.shape[0] // 2
    gate = total[:rows]
    return gate / (1.0 + jnp.exp(-gate)) * total[rows:]


def line_plan(count):
    even, odd, table = {}, {}, []
    for phase in range(1, count):
        for parity, names in ((0, even), (1, odd)):
            need = {}
            for i in range(count):
                rises = i % 2 == parity
                other = i + 1 if rises else i - 1
                shard = count - phase + i if rises else i - count + phase
                if 0 <= other < count and (i <= phase - 1 if rises else i >= count - phase):
                    need[i] = shard
            if not need:
                continue
            for number, held in enumerate(table):
                if all(held.get(i, shard) == shard for i, shard in need.items()):
                    break
            else:
                number = len(table)
                table.append({})
            table[number].update(need)
            names[phase] = number
    table.append({i: i for i in range(count)})
    return even, odd, [[held.get(i, i) for i in range(count)] for held in table]


def shared_kernel(table, x_ref, up_hbm, down_hbm, late_hbm, *rest):
    outs, rest = rest[: len(table)], rest[len(table) :]
    late_ref, up_ref, down_ref, hidden_ref, up_sem, down_sem, late_sem = rest
    rows, width = x_ref.shape
    share = outs[0].shape[0]
    hidden_width = up_ref.shape[2]
    count = chunk_count(width)
    size = width // count
    up_copies, down_copies = [], []
    for c in range(count):
        part = pl.ds(c * size, size)
        up_copies.append(pltpu.make_async_copy(up_hbm.at[part], up_ref.at[part], up_sem.at[c]))
        up_copies[-1].start()
    for c in range(count):
        part = pl.ds(c * size, size)
        down_copies.append(
            pltpu.make_async_copy(down_hbm.at[:, part], down_ref.at[:, part], down_sem.at[c])
        )
        down_copies[-1].start()
    late = pltpu.make_async_copy(late_hbm, late_ref, late_sem)
    late.start()
    twice = doubler()
    total = None
    for c in range(count):
        left = spread(x_ref[:, c * size : (c + 1) * size], twice)
        up_copies[c].wait()
        product = dot(left, up_ref.at[pl.ds(c * size, size)].reshape(2 * size, hidden_width)[...])
        total = product if total is None else total + product
    hidden_ref[...] = gated(total).astype(BF16)
    index = lax.axis_index("replica")
    picked = []
    for held in table:
        number = jnp.int32(0)
        for i, shard in enumerate(held):
            number = jnp.where(index == i, shard, number)
        picked.append(hidden_ref[pl.ds(pl.multiple_of(number * share, share), share), :])
    hidden = jnp.concatenate(picked, axis=0)
    for c in range(count):
        down_copies[c].wait()
        result = dot(hidden, down_ref[:, c * size : (c + 1) * size]).astype(BF16)
        for number, out in enumerate(outs):
            out[:, c * size : (c + 1) * size] = result[number * share : (number + 1) * share]
    late.wait()


def shared(tokens, up, down, late, table):
    rows, width = tokens.shape
    count = chunk_count(width)
    share = rows // len(table[0])
    vmem = pl.BlockSpec(memory_space=pltpu.VMEM)
    return pl.pallas_call(
        functools.partial(shared_kernel, table),
        out_shape=[pltpu.VMEM((share, width), BF16)] * len(table)
        + [pltpu.VMEM(late.shape, BF16)],
        in_specs=[vmem] + [pl.BlockSpec(memory_space=pltpu.HBM)] * 3,
        out_specs=[vmem] * (len(table) + 1),
        scratch_shapes=[
            pltpu.VMEM(up.shape, BF16),
            pltpu.VMEM(down.shape, BF16),
            pltpu.VMEM((rows, down.shape[0]), BF16),
            pltpu.SemaphoreType.DMA((count,)),
            pltpu.SemaphoreType.DMA((count,)),
            pltpu.SemaphoreType.DMA,
        ],
        compiler_params=pltpu.CompilerParams(vmem_limit_bytes=24 * MIB),
        cost_estimate=pl.CostEstimate(flops=3 * 10**9, bytes_accessed=25 * 10**6, transcendentals=0),
        name="shared",
    )(tokens, *in_hbm(up, down, late))


def expert_kernel(count, *refs):
    parts, up_ref, down_hbm, outs = refs[:count], refs[count], refs[count + 1], refs[count + 2 : -2]
    down_ref, down_sem = refs[-2:]
    copy = pltpu.make_async_copy(down_hbm, down_ref, down_sem)
    copy.start()
    lines, half = parts[0].shape
    hidden_width = up_ref.shape[2]
    pieces = chunk_count(half) if half % PIECE == 0 else 1
    size = half // pieces
    twice = doubler()
    totals = []
    for side in range(2):
        total = None
        for c in range(pieces):
            block = jnp.concatenate([part[:, c * size : (c + 1) * size] for part in parts], axis=0)
            left = spread(block, twice)
            start = side * half + c * size
            product = dot(left, up_ref.at[pl.ds(start, size)].reshape(2 * size, hidden_width)[...])
            total = product if total is None else total + product
        totals.append(total)
    height = count * lines
    slots = lines // 2

    def shifted(a, by):
        return pltpu.roll(a, by % a.shape[0], 0)

    top = lax.rem(iota((height, 1), 0), lines) < slots
    total = totals[0] + shifted(totals[1], -slots)
    hidden = gated(total)
    hidden = jnp.where(top, hidden, shifted(hidden, slots)).astype(BF16)
    copy.wait()
    for c in range(pieces):
        start = c * size
        first = dot(hidden, down_ref[:, start : start + size])
        second = dot(hidden, down_ref[:, half + start : half + start + size])
        both = jnp.where(top, first, second)
        for index in range(count):
            outs[index][:, start : start + size] = both[index * lines : (index + 1) * lines].astype(
                BF16
            )


def run_expert(parts, up, down):
    count = len(parts)
    vmem = pl.BlockSpec(memory_space=pltpu.VMEM)
    return pl.pallas_call(
        functools.partial(expert_kernel, count),
        out_shape=[jax.ShapeDtypeStruct(parts[0].shape, BF16)] * count,
        in_specs=[vmem] * (count + 1) + [pl.BlockSpec(memory_space=pltpu.HBM)],
        out_specs=[vmem] * count,
        scratch_shapes=[pltpu.VMEM(down.shape, BF16), pltpu.SemaphoreType.DMA],
        compiler_params=pltpu.CompilerParams(vmem_limit_bytes=32 * MIB),
        cost_estimate=pl.CostEstimate(flops=6 * 10**10, bytes_accessed=13 * 10**6, transcendentals=0),
        name="routed",
    )(*parts, up, *in_hbm(down))


def seat_kernel(count, capacity, source_ref, *refs):
    parts, keep_ref, send_ref = refs[:count], refs[count], refs[count + 1]
    lines, half = parts[0].shape
    slots = lines // 2
    me = lax.axis_index("expert")
    side = lax.rem(lax.axis_index("replica"), 2)
    shape = (count * capacity, count * lines)
    seat, line = iota(shape, 0), iota(shape, 1)
    within = lax.rem(line, lines)
    slot = lax.rem(within, slots)
    expert = me ^ (line // lines)
    home = jnp.zeros(shape, I32)
    for index in range(count):
        home = jnp.where(expert == source_ref[index], index, home)
    target = jnp.where(slot < capacity, expert * capacity + slot, home * capacity + slot - capacity)
    here = (target == seat).astype(F32)
    second = (within >= slots).astype(I32)
    keep = jnp.where(second == side, here, 0.0).astype(BF16)
    send = jnp.where(second == side, 0.0, here).astype(BF16)
    pieces = chunk_count(half) if half % PIECE == 0 else 1
    size = half // pieces
    for c in range(pieces):
        cols = slice(c * size, (c + 1) * size)
        block = jnp.concatenate([part[:, cols] for part in parts], axis=0)
        keep_ref[:, cols] = dot(keep, block).astype(BF16)
        send_ref[:, cols] = dot(send, block).astype(BF16)


def seat_answers(parts, copy_source, capacity):
    count = len(parts)
    vmem = pl.BlockSpec(memory_space=pltpu.VMEM)
    shape = jax.ShapeDtypeStruct((count * capacity, parts[0].shape[1]), BF16)
    return pl.pallas_call(
        functools.partial(seat_kernel, count, capacity),
        out_shape=[shape, shape],
        in_specs=[pl.BlockSpec(memory_space=pltpu.SMEM)] + [vmem] * count,
        out_specs=[vmem, vmem],
        compiler_params=pltpu.CompilerParams(vmem_limit_bytes=16 * MIB),
        cost_estimate=pl.CostEstimate(flops=10**8, bytes_accessed=2 * 10**6, transcendentals=0),
        name="seats",
    )(copy_source, *parts)


def mix_kernel(own_ref, even_ref, odd_ref, gate_ref, mine_ref, other_ref, out_ref):
    side = lax.rem(lax.axis_index("replica"), 2)
    seats, half = mine_ref.shape
    gates = gate_ref[:, :seats]
    high = gates.astype(BF16)
    left = gates - high.astype(F32)
    middle = left.astype(BF16)
    low = (left - middle.astype(F32)).astype(BF16)
    for position in range(2):
        cols = slice(position * half, (position + 1) * half)
        answers = jnp.where(side == position, mine_ref[...], other_ref[...])
        routed = dot(high, answers) + dot(middle, answers) + dot(low, answers)
        base = own_ref[:, cols].astype(F32) + even_ref[:, cols].astype(F32) + odd_ref[:, cols].astype(F32)
        out_ref[:, cols] = (base + routed).astype(BF16)


def mix(own, even, odd, gates, mine, other):
    vmem = pl.BlockSpec(memory_space=pltpu.VMEM)
    return pl.pallas_call(
        mix_kernel,
        out_shape=jax.ShapeDtypeStruct(own.shape, BF16),
        in_specs=[vmem] * 6,
        out_specs=vmem,
        compiler_params=pltpu.CompilerParams(vmem_limit_bytes=16 * MIB),
        cost_estimate=pl.CostEstimate(flops=10**8, bytes_accessed=2 * 10**6, transcendentals=0),
        name="mix",
    )(own, even, odd, gates, mine, other)


def swap(array, axis, distance):
    pairs = [(i, i ^ distance) for i in range(lax.axis_size(axis))]
    return lax.ppermute(array, axis, pairs)


def add(a, b):
    return (a.astype(F32) + b.astype(F32)).astype(BF16)


def shards(
    tokens,
    route_ids,
    route_gates,
    copy_source,
    copy_share,
    w_gate_up,
    w_down,
    shared_gate_up,
    shared_down,
):
    experts = lax.axis_size("expert")
    replicas = lax.axis_size("replica")
    rows = tokens.shape[0]
    capacity = max(2, rows * 3 // 64)
    even, odd, table = line_plan(replicas)
    even_pairs = [(i, i ^ 1) for i in range(replicas)]
    odd_pairs = [(i, i + 1 if i % 2 else i - 1) for i in range(1, replicas - 1)]
    gates, tokens, *outgoing = plan(
        route_ids, route_gates, copy_source, copy_share, tokens, experts, capacity
    )
    incoming = [outgoing[0]] + [swap(outgoing[d], "expert", d) for d in range(1, experts)]
    *parts, up = shared(tokens, shared_gate_up, shared_down, w_gate_up[0], table)
    got_even = got_odd = None

    def phase(number, got_even, got_odd):
        send_even, send_odd = parts[even[number]], None
        if got_odd is not None:
            send_even = add(send_even, got_odd)
        elif got_even is not None:
            send_even, got_even = lax.optimization_barrier((send_even, got_even))
        if number in odd:
            send_odd = add(parts[odd[number]], got_even)
        got_even = lax.ppermute(send_even, "replica", even_pairs)
        got_odd = lax.ppermute(send_odd, "replica", odd_pairs) if number in odd else None
        return got_even, got_odd

    got_even, got_odd = phase(1, None, None)
    results = run_expert(incoming, up, w_down[0])
    answers = [results[0]] + [swap(results[d], "expert", d) for d in range(1, experts)]
    if replicas > 2:
        near = min(2, experts - 1)
        got_even, answers[near] = lax.optimization_barrier((got_even, answers[near]))
        got_even, got_odd = phase(2, got_even, got_odd)
    keep, send = seat_answers(answers, copy_source, capacity)
    got = swap(send, "replica", 1)
    for number in range(3, replicas):
        got_even, got_odd, keep = lax.optimization_barrier((got_even, got_odd, keep))
        got_even, got_odd = phase(number, got_even, got_odd)
    mine = add(keep, got)
    distance = 2
    while distance < replicas:
        mine = add(mine, swap(mine, "replica", distance))
        distance *= 2
    other = swap(mine, "replica", 1)
    share = rows // replicas
    own_gates = lax.dynamic_slice_in_dim(gates, lax.axis_index("replica") * share, share, 0)
    if got_odd is None:
        got_odd = jnp.zeros_like(got_even)
    return mix(parts[-1], got_even, got_odd, own_gates, mine, other)


def solution(mesh):
    return jax.shard_map(
        shards,
        mesh=mesh,
        in_specs=(
            P(("group", "expert"), None),
            P(("group", "expert"), None),
            P(("group", "expert"), None),
            P("group"),
            P("group"),
            P("expert", None, None, "replica"),
            P("expert", "replica", None),
            P(None, None, "replica"),
            P("replica", None),
        ),
        out_specs=P(("group", "expert", "replica"), None),
        check_vma=False,
    )
```

```python
import functools

import jax
import jax.numpy as jnp
from jax import lax
from jax.experimental import pallas as pl
from jax.experimental.pallas import tpu as pltpu
from jax.sharding import PartitionSpec as P

BF16 = jnp.bfloat16
F32 = jnp.float32
I32 = jnp.int32
PIECE = 256
MIB = 1 << 20


def iota(shape, dim):
    return lax.broadcasted_iota(I32, shape, dim)


def dot(a, b):
    return jnp.dot(a, b, preferred_element_type=F32)


def in_hbm(*arrays):
    return [pltpu.with_memory_space_constraint(array, pltpu.HBM) for array in arrays]


def chunk_count(width):
    for count in (4, 2, 1):
        if width % (count * PIECE) == 0:
            return count
    raise ValueError(width)


def scatter_rows(outs, columns, values):
    first = 0
    for out in outs:
        last = first + out.shape[0]
        out[:, columns] = values[first:last].astype(BF16)
        first = last


def bundles(experts, lines, width):
    half = max(1, experts // 2)
    heights = [lines] * half + [lines * (experts - half)] * (experts > half)
    return [pltpu.VMEM((height, width), BF16) for height in heights]


def plan_kernel(
    experts, capacity, share_hbm, source_hbm, ids_hbm, gates_hbm, tokens_hbm, up_hbm, gate_out, tokens_ref, head_ref, *rest
):
    *outs, share_ref, source_ref, ids_ref, gates_ref, sems = rest
    copies = [
        pltpu.make_async_copy(source, target, sems.at[number])
        for number, (source, target) in enumerate(
            [
                (ids_hbm, ids_ref),
                (share_hbm, share_ref),
                (source_hbm, source_ref),
                (gates_hbm, gates_ref),
                (tokens_hbm, tokens_ref),
                (up_hbm.at[pl.ds(0, head_ref.shape[0])], head_ref),
            ]
        )
    ]
    for copy in copies:
        copy.start()
    for copy in copies[:4]:
        copy.wait()
    ids = ids_ref[...]
    gates = gates_ref[...]
    top, rows = ids.shape
    me = lax.axis_index("expert")
    inside = ids < experts
    limit = jnp.zeros_like(ids)
    home = jnp.zeros_like(ids)
    for index in range(experts):
        limit = jnp.where(ids == index, share_ref[index], limit)
        home = jnp.where(ids == source_ref[index], index, home)
    by_copy = inside & (iota((top, rows), 1) < limit)
    holder = jnp.where(by_copy, home, ids)
    members = [jnp.where(inside & (holder == index), 1.0, 0.0) for index in range(experts)]
    earlier = jnp.where(iota((rows, rows), 0) < iota((rows, rows), 1), 1.0, 0.0).astype(BF16)
    rank = jnp.zeros((top, rows), F32)
    for index in range(experts):
        member = members[index]
        counts = jnp.broadcast_to(jnp.sum(member, axis=0, keepdims=True), (8, rows))
        running = dot(counts.astype(BF16), earlier)[:1]
        lines = []
        for k in range(top):
            lines.append(running)
            running = running + member[k : k + 1]
        rank = rank + member * jnp.concatenate(lines, axis=0)
    rank = rank.astype(I32)
    served = inside & (rank < capacity)
    slots = 2 * capacity
    place = jnp.where(served, ids * slots + rank + jnp.where(by_copy, capacity, 0), -1)
    seat = jnp.where(served, holder * capacity + rank, -1)
    seats = jnp.zeros((rows, rows), F32)
    for k in range(top):
        seats = seats + jnp.where(seat[k : k + 1] == iota((rows, rows), 0), gates[k : k + 1], 0.0)
    gate_out[...] = seats.T
    height = experts * 2 * slots
    line = iota((height, 1), 0)
    within = lax.rem(line, 2 * slots)
    wanted = (me ^ (line // (2 * slots))) * slots + lax.rem(within, slots)
    pick = jnp.zeros((height, rows), F32)
    for k in range(top):
        pick = pick + jnp.where(place[k : k + 1] == wanted, 1.0, 0.0)
    first = jnp.where(within < slots, pick, 0.0).astype(BF16)
    second = jnp.where(within < slots, 0.0, pick).astype(BF16)
    copies[4].wait()
    half = tokens_ref.shape[1] // 2
    step = half // chunk_count(half) if half % PIECE == 0 else half
    for start in range(0, half, step):
        picked = dot(first, tokens_ref[:, start : start + step]) + dot(
            second, tokens_ref[:, half + start : half + start + step]
        )
        scatter_rows(outs, slice(start, start + step), picked)
    copies[5].wait()


def plan(route_ids, route_gates, copy_source, copy_share, tokens, up, experts, capacity):
    rows, width = tokens.shape
    sent = bundles(experts, 4 * capacity, width // 2)
    vmem = pl.BlockSpec(memory_space=pltpu.VMEM)
    hbm = pl.BlockSpec(memory_space=pltpu.HBM)
    return pl.pallas_call(
        functools.partial(plan_kernel, experts, capacity),
        out_shape=[
            pltpu.VMEM((rows, rows), F32),
            pltpu.VMEM((rows, width), BF16),
            pltpu.VMEM((width // 2,) + up.shape[1:], BF16),
        ]
        + sent,
        in_specs=[hbm] * 6,
        out_specs=[vmem] * (len(sent) + 3),
        scratch_shapes=[
            pltpu.SMEM(copy_share.shape, I32),
            pltpu.SMEM(copy_source.shape, I32),
            pltpu.VMEM(route_ids.shape[::-1], I32),
            pltpu.VMEM(route_gates.shape[::-1], F32),
            pltpu.SemaphoreType.DMA((6,)),
        ],
        compiler_params=pltpu.CompilerParams(vmem_limit_bytes=16 * MIB),
        cost_estimate=pl.CostEstimate(flops=10**8, bytes_accessed=4 * 10**6, transcendentals=0),
        name="plan",
    )(*in_hbm(copy_share, copy_source, route_ids.T, route_gates.T, tokens, up))


def doubler():
    shape = (PIECE, 2 * PIECE)
    return jnp.where(iota(shape, 1) // 2 == iota(shape, 0), 1.0, 0.0).astype(BF16)


def spread(block, twice):
    parts = []
    for start in range(0, block.shape[1], PIECE):
        both = dot(block[:, start : start + PIECE], twice)
        even = lax.rem(iota(both.shape, 1), 2) == 0
        gate = jnp.where(even, both, 0.0).astype(BF16)
        up = jnp.where(even, 0.0, both).astype(BF16)
        parts.append(jnp.concatenate([gate, up], axis=0))
    return jnp.concatenate(parts, axis=1)


def gated(total):
    rows = total.shape[0] // 2
    gate = total[:rows]
    return gate / (1.0 + jnp.exp(-gate)) * total[rows:]


def line_plan(count):
    even, odd, table = {}, {}, []
    for phase in range(1, count):
        for parity, names in ((0, even), (1, odd)):
            need = {}
            for i in range(count):
                rises = i % 2 == parity
                other = i + 1 if rises else i - 1
                shard = count - phase + i if rises else i - count + phase
                if 0 <= other < count and (i <= phase - 1 if rises else i >= count - phase):
                    need[i] = shard
            if not need:
                continue
            for number, held in enumerate(table):
                if all(held.get(i, shard) == shard for i, shard in need.items()):
                    break
            else:
                number = len(table)
                table.append({})
            table[number].update(need)
            names[phase] = number
    table.append({i: i for i in range(count)})
    return even, odd, [[held.get(i, i) for i in range(count)] for held in table]


def shared_kernel(table, x_ref, head_ref, up_hbm, down_hbm, *rest):
    outs, rest = rest[: len(table)], rest[len(table) :]
    up_ref, down_ref, hidden_ref, up_sem, down_sem = rest
    rows, width = x_ref.shape
    share = outs[0].shape[0]
    hidden_width = up_ref.shape[2]
    count = chunk_count(width)
    size = width // count
    up_copies, down_copies = [], []
    known = head_ref.shape[0] // size
    for c in range(count - known):
        there, here = pl.ds((known + c) * size, size), pl.ds(c * size, size)
        up_copies.append(pltpu.make_async_copy(up_hbm.at[there], up_ref.at[here], up_sem.at[c]))
        up_copies[-1].start()
    for c in range(count):
        part = pl.ds(c * size, size)
        down_copies.append(
            pltpu.make_async_copy(down_hbm.at[:, part], down_ref.at[:, part], down_sem.at[c])
        )
        down_copies[-1].start()
    twice = doubler()
    total = None
    for c in range(count):
        left = spread(x_ref[:, c * size : (c + 1) * size], twice)
        source, place = head_ref, c
        if c >= known:
            source, place = up_ref, c - known
            up_copies[place].wait()
        weights = source.at[pl.ds(place * size, size)].reshape(2 * size, hidden_width)[...]
        product = dot(left, weights)
        total = product if total is None else total + product
    hidden_ref[...] = gated(total).astype(BF16)
    index = lax.axis_index("replica")
    picked = []
    for held in table:
        number = jnp.int32(0)
        for i, shard in enumerate(held):
            number = jnp.where(index == i, shard, number)
        picked.append(hidden_ref[pl.ds(pl.multiple_of(number * share, share), share), :])
    hidden = jnp.concatenate(picked, axis=0)
    for c in range(count):
        down_copies[c].wait()
        result = dot(hidden, down_ref[:, c * size : (c + 1) * size]).astype(BF16)
        for number, out in enumerate(outs):
            out[:, c * size : (c + 1) * size] = result[number * share : (number + 1) * share]


def shared(tokens, head, up, down, table):
    rows, width = tokens.shape
    count = chunk_count(width)
    share = rows // len(table[0])
    vmem = pl.BlockSpec(memory_space=pltpu.VMEM)
    return pl.pallas_call(
        functools.partial(shared_kernel, table),
        out_shape=[pltpu.VMEM((share, width), BF16)] * len(table),
        in_specs=[vmem] * 2 + [pl.BlockSpec(memory_space=pltpu.HBM)] * 2,
        out_specs=[vmem] * len(table),
        scratch_shapes=[
            pltpu.VMEM((width - head.shape[0],) + up.shape[1:], BF16),
            pltpu.VMEM(down.shape, BF16),
            pltpu.VMEM((rows, down.shape[0]), BF16),
            pltpu.SemaphoreType.DMA((count,)),
            pltpu.SemaphoreType.DMA((count,)),
        ],
        compiler_params=pltpu.CompilerParams(vmem_limit_bytes=18 * MIB),
        cost_estimate=pl.CostEstimate(flops=3 * 10**9, bytes_accessed=25 * 10**6, transcendentals=0),
        name="shared",
    )(tokens, head, *in_hbm(up, down))


def expert_kernel(count, *refs):
    parts, up_ref, down_ref, outs = refs[:count], refs[count], refs[count + 1], refs[count + 2 :]
    lines, half = parts[0].shape
    hidden_width = up_ref.shape[2]
    pieces = chunk_count(half) if half % PIECE == 0 else 1
    size = half // pieces
    twice = doubler()
    totals = []
    for side in range(2):
        total = None
        for c in range(pieces):
            block = jnp.concatenate([part[:, c * size : (c + 1) * size] for part in parts], axis=0)
            left = spread(block, twice)
            start = side * half + c * size
            product = dot(left, up_ref.at[pl.ds(start, size)].reshape(2 * size, hidden_width)[...])
            total = product if total is None else total + product
        totals.append(total)
    height = count * lines
    slots = lines // 2

    def shifted(a, by):
        return pltpu.roll(a, by % a.shape[0], 0)

    top = lax.rem(iota((height, 1), 0), lines) < slots
    total = totals[0] + shifted(totals[1], -slots)
    hidden = gated(total)
    hidden = jnp.where(top, hidden, shifted(hidden, slots)).astype(BF16)
    for c in range(pieces):
        start = c * size
        first = dot(hidden, down_ref[:, start : start + size])
        second = dot(hidden, down_ref[:, half + start : half + start + size])
        scatter_rows(outs, slice(start, start + size), jnp.where(top, first, second))


def run_expert(parts, up, down):
    count = len(parts)
    sent = bundles(count, *parts[0].shape)
    vmem = pl.BlockSpec(memory_space=pltpu.VMEM)
    return pl.pallas_call(
        functools.partial(expert_kernel, count),
        out_shape=sent,
        in_specs=[vmem] * (count + 2),
        out_specs=[vmem] * len(sent),
        compiler_params=pltpu.CompilerParams(vmem_limit_bytes=16 * MIB),
        cost_estimate=pl.CostEstimate(flops=10**8, bytes_accessed=13 * 10**6, transcendentals=0),
        name="routed",
    )(*parts, up, down)


def seat_kernel(count, capacity, source_ref, *refs):
    parts, keep_ref, send_ref = refs[:count], refs[count], refs[count + 1]
    lines, half = parts[0].shape
    slots = lines // 2
    me = lax.axis_index("expert")
    side = lax.rem(lax.axis_index("replica"), 2)
    shape = (count * capacity, count * lines)
    seat, line = iota(shape, 0), iota(shape, 1)
    within = lax.rem(line, lines)
    slot = lax.rem(within, slots)
    expert = me ^ (line // lines)
    home = jnp.zeros(shape, I32)
    for index in range(count):
        home = jnp.where(expert == source_ref[index], index, home)
    target = jnp.where(slot < capacity, expert * capacity + slot, home * capacity + slot - capacity)
    here = (target == seat).astype(F32)
    second = (within >= slots).astype(I32)
    keep = jnp.where(second == side, here, 0.0).astype(BF16)
    send = jnp.where(second == side, 0.0, here).astype(BF16)
    pieces = chunk_count(half) if half % PIECE == 0 else 1
    size = half // pieces
    for c in range(pieces):
        cols = slice(c * size, (c + 1) * size)
        block = jnp.concatenate([part[:, cols] for part in parts], axis=0)
        keep_ref[:, cols] = dot(keep, block).astype(BF16)
        send_ref[:, cols] = dot(send, block).astype(BF16)


def seat_answers(parts, copy_source, capacity):
    count = len(parts)
    vmem = pl.BlockSpec(memory_space=pltpu.VMEM)
    shape = jax.ShapeDtypeStruct((count * capacity, parts[0].shape[1]), BF16)
    return pl.pallas_call(
        functools.partial(seat_kernel, count, capacity),
        out_shape=[shape, shape],
        in_specs=[pl.BlockSpec(memory_space=pltpu.SMEM)] + [vmem] * count,
        out_specs=[vmem, vmem],
        compiler_params=pltpu.CompilerParams(vmem_limit_bytes=16 * MIB),
        cost_estimate=pl.CostEstimate(flops=10**7, bytes_accessed=10**5, transcendentals=0),
        name="seats",
    )(copy_source, *parts)


def mix_kernel(own_ref, even_ref, odd_ref, gate_ref, mine_ref, other_ref, out_ref):
    side = lax.rem(lax.axis_index("replica"), 2)
    seats, half = mine_ref.shape
    gates = gate_ref[:, :seats]
    high = gates.astype(BF16)
    left = gates - high.astype(F32)
    middle = left.astype(BF16)
    low = (left - middle.astype(F32)).astype(BF16)
    for position in range(2):
        cols = slice(position * half, (position + 1) * half)
        answers = jnp.where(side == position, mine_ref[...], other_ref[...])
        routed = dot(high, answers) + dot(middle, answers) + dot(low, answers)
        base = own_ref[:, cols].astype(F32) + even_ref[:, cols].astype(F32) + odd_ref[:, cols].astype(F32)
        out_ref[:, cols] = (base + routed).astype(BF16)


def mix(own, even, odd, gates, mine, other):
    vmem = pl.BlockSpec(memory_space=pltpu.VMEM)
    return pl.pallas_call(
        mix_kernel,
        out_shape=jax.ShapeDtypeStruct(own.shape, BF16),
        in_specs=[vmem] * 6,
        out_specs=vmem,
        compiler_params=pltpu.CompilerParams(vmem_limit_bytes=16 * MIB),
        cost_estimate=pl.CostEstimate(flops=10**8, bytes_accessed=2 * 10**6, transcendentals=0),
        name="mix",
    )(own, even, odd, gates, mine, other)


def swap(array, axis, distance):
    pairs = [(i, i ^ distance) for i in range(lax.axis_size(axis))]
    return lax.ppermute(array, axis, pairs)


def exchange(blocks, axis):
    count = len(blocks)
    if count == 1:
        return blocks
    half = count // 2
    high = blocks[half] if half == 1 else jnp.concatenate(blocks[half:], axis=0)
    got = jnp.split(swap(high, axis, half), half, axis=0)
    return exchange(blocks[:half], axis) + exchange(got, axis)


def exchange_bundles(sent, axis, then):
    count = lax.axis_size(axis)
    half = count // 2
    if half == 0:
        return list(sent)
    got = swap(sent[half], axis, half)
    near, got = then(exchange(list(sent[:half]), axis), got)
    return near + exchange(jnp.split(got, half, axis=0), axis)


def add(a, b):
    return (a.astype(F32) + b.astype(F32)).astype(BF16)


def shards(
    tokens,
    route_ids,
    route_gates,
    copy_source,
    copy_share,
    w_gate_up,
    w_down,
    shared_gate_up,
    shared_down,
):
    experts = lax.axis_size("expert")
    replicas = lax.axis_size("replica")
    rows = tokens.shape[0]
    capacity = max(2, rows * 3 // 64)
    even, odd, table = line_plan(replicas)
    even_pairs = [(i, i ^ 1) for i in range(replicas)]
    odd_pairs = [(i, i + 1 if i % 2 else i - 1) for i in range(1, replicas - 1)]
    gates, tokens, head, *outgoing = plan(
        route_ids, route_gates, copy_source, copy_share, tokens, shared_gate_up, experts, capacity
    )
    parts = shared(tokens, head, shared_gate_up, shared_down, table)

    def after_shared(near, far):
        far, _ = lax.optimization_barrier((far, parts[-1]))
        return near, far

    incoming = exchange_bundles(outgoing, "expert", after_shared)
    sums = [None, None]

    def phase(number, *after):
        got_even, got_odd = sums
        if got_odd is not None:
            got_even, got_odd, *_ = lax.optimization_barrier((got_even, got_odd, *after))
        elif got_even is not None and after:
            got_even, *_ = lax.optimization_barrier((got_even, *after))
        send_even, send_odd = parts[even[number]], None
        if got_odd is not None:
            send_even = add(send_even, got_odd)
        elif got_even is not None:
            send_even, got_even = lax.optimization_barrier((send_even, got_even))
        if number in odd:
            send_odd = add(parts[odd[number]], got_even)
        sums[0] = lax.ppermute(send_even, "replica", even_pairs)
        sums[1] = lax.ppermute(send_odd, "replica", odd_pairs) if number in odd else None
        return [send_even] if send_odd is None else [send_even, send_odd]

    phase(1)
    results = run_expert(incoming, w_gate_up[0], w_down[0])

    def after_first(near, far):
        if replicas > 2:
            far, *_ = lax.optimization_barrier((far, *phase(2, near[-1])))
        return near, far

    answers = exchange_bundles(results, "expert", after_first)
    keep, send = seat_answers(answers, copy_source, capacity)
    number, distance = 3, 2
    got, mine = swap(send, "replica", 1), keep
    while True:
        if number < replicas:
            got, *_ = lax.optimization_barrier((got, *phase(number)))
            number += 1
        mine = add(mine, got)
        if distance >= replicas:
            break
        got = swap(mine, "replica", distance)
        distance *= 2
    other = swap(mine, "replica", 1)
    for rest in range(number, replicas):
        phase(rest, mine)
    got_even, got_odd = sums
    share = rows // replicas
    own_gates = lax.dynamic_slice_in_dim(gates, lax.axis_index("replica") * share, share, 0)
    if got_odd is None:
        got_odd = jnp.zeros_like(got_even)
    return mix(parts[-1], got_even, got_odd, own_gates, mine, other)


def solution(mesh):
    return jax.shard_map(
        shards,
        mesh=mesh,
        in_specs=(
            P(("group", "expert"), None),
            P(("group", "expert"), None),
            P(("group", "expert"), None),
            P("group"),
            P("group"),
            P("expert", None, None, "replica"),
            P("expert", "replica", None),
            P(None, None, "replica"),
            P("replica", None),
        ),
        out_specs=P(("group", "expert", "replica"), None),
        check_vma=False,
    )
```

```python
import functools

import jax
import jax.numpy as jnp
from jax import lax
from jax.experimental import pallas as pl
from jax.experimental.pallas import tpu as pltpu
from jax.sharding import PartitionSpec as P

BF16 = jnp.bfloat16
F32 = jnp.float32
I32 = jnp.int32
PIECE = 256
MIB = 1 << 20


def iota(shape, dim):
    return lax.broadcasted_iota(I32, shape, dim)


def dot(a, b):
    return jnp.dot(a, b, preferred_element_type=F32)


def in_hbm(*arrays):
    return [pltpu.with_memory_space_constraint(array, pltpu.HBM) for array in arrays]


def chunk_count(width):
    for count in (4, 2, 1):
        if width % (count * PIECE) == 0:
            return count
    raise ValueError(width)


def scatter_rows(outs, columns, values):
    first = 0
    for out in outs:
        last = first + out.shape[0]
        out[:, columns] = values[first:last].astype(BF16)
        first = last


def bundles(experts, lines, width):
    half = max(1, experts // 2)
    heights = [lines] * half + [lines * (experts - half)] * (experts > half)
    return [pltpu.VMEM((height, width), BF16) for height in heights]


def plan_kernel(
    experts, capacity, share_hbm, source_hbm, ids_hbm, gates_hbm, tokens_hbm, up_hbm, gate_out, tokens_ref, head_ref, *rest
):
    *outs, share_ref, source_ref, ids_ref, gates_ref, sems = rest
    copies = [
        pltpu.make_async_copy(source, target, sems.at[number])
        for number, (source, target) in enumerate(
            [
                (ids_hbm, ids_ref),
                (share_hbm, share_ref),
                (source_hbm, source_ref),
                (gates_hbm, gates_ref),
                (tokens_hbm, tokens_ref),
                (up_hbm.at[pl.ds(0, head_ref.shape[0])], head_ref),
            ]
        )
    ]
    for copy in copies:
        copy.start()
    for copy in copies[:4]:
        copy.wait()
    ids = ids_ref[...]
    gates = gates_ref[...]
    top, rows = ids.shape
    me = lax.axis_index("expert")
    inside = ids < experts
    limit = jnp.zeros_like(ids)
    home = jnp.zeros_like(ids)
    for index in range(experts):
        limit = jnp.where(ids == index, share_ref[index], limit)
        home = jnp.where(ids == source_ref[index], index, home)
    by_copy = inside & (iota((top, rows), 1) < limit)
    holder = jnp.where(by_copy, home, ids)
    members = [jnp.where(inside & (holder == index), 1.0, 0.0) for index in range(experts)]
    earlier = jnp.where(iota((rows, rows), 0) < iota((rows, rows), 1), 1.0, 0.0).astype(BF16)
    rank = jnp.zeros((top, rows), F32)
    for index in range(experts):
        member = members[index]
        counts = jnp.broadcast_to(jnp.sum(member, axis=0, keepdims=True), (8, rows))
        running = dot(counts.astype(BF16), earlier)[:1]
        lines = []
        for k in range(top):
            lines.append(running)
            running = running + member[k : k + 1]
        rank = rank + member * jnp.concatenate(lines, axis=0)
    rank = rank.astype(I32)
    served = inside & (rank < capacity)
    slots = 2 * capacity
    place = jnp.where(served, ids * slots + rank + jnp.where(by_copy, capacity, 0), -1)
    seat = jnp.where(served, holder * capacity + rank, -1)
    seats = jnp.zeros((rows, rows), F32)
    for k in range(top):
        seats = seats + jnp.where(seat[k : k + 1] == iota((rows, rows), 0), gates[k : k + 1], 0.0)
    gate_out[...] = seats.T
    height = experts * 2 * slots
    line = iota((height, 1), 0)
    within = lax.rem(line, 2 * slots)
    wanted = (me ^ (line // (2 * slots))) * slots + lax.rem(within, slots)
    pick = jnp.zeros((height, rows), F32)
    for k in range(top):
        pick = pick + jnp.where(place[k : k + 1] == wanted, 1.0, 0.0)
    first = jnp.where(within < slots, pick, 0.0).astype(BF16)
    second = jnp.where(within < slots, 0.0, pick).astype(BF16)
    copies[4].wait()
    half = tokens_ref.shape[1] // 2
    step = half // chunk_count(half) if half % PIECE == 0 else half
    for start in range(0, half, step):
        picked = dot(first, tokens_ref[:, start : start + step]) + dot(
            second, tokens_ref[:, half + start : half + start + step]
        )
        scatter_rows(outs, slice(start, start + step), picked)
    copies[5].wait()


def plan(route_ids, route_gates, copy_source, copy_share, tokens, up, experts, capacity):
    rows, width = tokens.shape
    sent = bundles(experts, 4 * capacity, width // 2)
    vmem = pl.BlockSpec(memory_space=pltpu.VMEM)
    hbm = pl.BlockSpec(memory_space=pltpu.HBM)
    return pl.pallas_call(
        functools.partial(plan_kernel, experts, capacity),
        out_shape=[
            pltpu.VMEM((rows, rows), F32),
            pltpu.VMEM((rows, width), BF16),
            pltpu.VMEM((width // 2,) + up.shape[1:], BF16),
        ]
        + sent,
        in_specs=[hbm] * 6,
        out_specs=[vmem] * (len(sent) + 3),
        scratch_shapes=[
            pltpu.SMEM(copy_share.shape, I32),
            pltpu.SMEM(copy_source.shape, I32),
            pltpu.VMEM(route_ids.shape[::-1], I32),
            pltpu.VMEM(route_gates.shape[::-1], F32),
            pltpu.SemaphoreType.DMA((6,)),
        ],
        compiler_params=pltpu.CompilerParams(vmem_limit_bytes=16 * MIB),
        cost_estimate=pl.CostEstimate(flops=10**8, bytes_accessed=4 * 10**6, transcendentals=0),
        name="plan",
    )(*in_hbm(copy_share, copy_source, route_ids.T, route_gates.T, tokens, up))


def doubler():
    shape = (PIECE, 2 * PIECE)
    return jnp.where(iota(shape, 1) // 2 == iota(shape, 0), 1.0, 0.0).astype(BF16)


def spread(block, twice):
    parts = []
    for start in range(0, block.shape[1], PIECE):
        both = dot(block[:, start : start + PIECE], twice)
        even = lax.rem(iota(both.shape, 1), 2) == 0
        gate = jnp.where(even, both, 0.0).astype(BF16)
        up = jnp.where(even, 0.0, both).astype(BF16)
        parts.append(jnp.concatenate([gate, up], axis=0))
    return jnp.concatenate(parts, axis=1)


def gated(total):
    rows = total.shape[0] // 2
    gate = total[:rows]
    return gate / (1.0 + jnp.exp(-gate)) * total[rows:]


def line_plan(count):
    even, odd, table = {}, {}, []
    for phase in range(1, count):
        for parity, names in ((0, even), (1, odd)):
            need = {}
            for i in range(count):
                rises = i % 2 == parity
                other = i + 1 if rises else i - 1
                shard = count - phase + i if rises else i - count + phase
                if 0 <= other < count and (i <= phase - 1 if rises else i >= count - phase):
                    need[i] = shard
            if not need:
                continue
            for number, held in enumerate(table):
                if all(held.get(i, shard) == shard for i, shard in need.items()):
                    break
            else:
                number = len(table)
                table.append({})
            table[number].update(need)
            names[phase] = number
    table.append({i: i for i in range(count)})
    return even, odd, [[held.get(i, i) for i in range(count)] for held in table]


def shared_kernel(table, x_ref, head_ref, up_hbm, down_hbm, *rest):
    outs, rest = rest[: len(table)], rest[len(table) :]
    up_ref, down_ref, hidden_ref, up_sem, down_sem = rest
    rows, width = x_ref.shape
    share = outs[0].shape[0]
    hidden_width = up_ref.shape[2]
    count = chunk_count(width)
    size = width // count
    up_copies, down_copies = [], []
    known = head_ref.shape[0] // size
    for c in range(count - known):
        there, here = pl.ds((known + c) * size, size), pl.ds(c * size, size)
        up_copies.append(pltpu.make_async_copy(up_hbm.at[there], up_ref.at[here], up_sem.at[c]))
        up_copies[-1].start()
    for c in range(count):
        part = pl.ds(c * size, size)
        down_copies.append(
            pltpu.make_async_copy(down_hbm.at[:, part], down_ref.at[:, part], down_sem.at[c])
        )
        down_copies[-1].start()
    twice = doubler()
    total = None
    for c in range(count):
        left = spread(x_ref[:, c * size : (c + 1) * size], twice)
        source, place = head_ref, c
        if c >= known:
            source, place = up_ref, c - known
            up_copies[place].wait()
        weights = source.at[pl.ds(place * size, size)].reshape(2 * size, hidden_width)[...]
        product = dot(left, weights)
        total = product if total is None else total + product
    hidden_ref[...] = gated(total).astype(BF16)
    index = lax.axis_index("replica")
    picked = []
    for held in table:
        number = jnp.int32(0)
        for i, shard in enumerate(held):
            number = jnp.where(index == i, shard, number)
        picked.append(hidden_ref[pl.ds(pl.multiple_of(number * share, share), share), :])
    hidden = jnp.concatenate(picked, axis=0)
    for c in range(count):
        down_copies[c].wait()
        result = dot(hidden, down_ref[:, c * size : (c + 1) * size]).astype(BF16)
        for number, out in enumerate(outs):
            out[:, c * size : (c + 1) * size] = result[number * share : (number + 1) * share]


def shared(tokens, head, up, down, table):
    rows, width = tokens.shape
    count = chunk_count(width)
    share = rows // len(table[0])
    vmem = pl.BlockSpec(memory_space=pltpu.VMEM)
    return pl.pallas_call(
        functools.partial(shared_kernel, table),
        out_shape=[pltpu.VMEM((share, width), BF16)] * len(table),
        in_specs=[vmem] * 2 + [pl.BlockSpec(memory_space=pltpu.HBM)] * 2,
        out_specs=[vmem] * len(table),
        scratch_shapes=[
            pltpu.VMEM((width - head.shape[0],) + up.shape[1:], BF16),
            pltpu.VMEM(down.shape, BF16),
            pltpu.VMEM((rows, down.shape[0]), BF16),
            pltpu.SemaphoreType.DMA((count,)),
            pltpu.SemaphoreType.DMA((count,)),
        ],
        compiler_params=pltpu.CompilerParams(vmem_limit_bytes=18 * MIB),
        cost_estimate=pl.CostEstimate(flops=3 * 10**9, bytes_accessed=25 * 10**6, transcendentals=0),
        name="shared",
    )(tokens, head, *in_hbm(up, down))


def expert_kernel(count, *refs):
    parts, up_ref, down_ref, outs = refs[:count], refs[count], refs[count + 1], refs[count + 2 :]
    lines, half = parts[0].shape
    hidden_width = up_ref.shape[2]
    pieces = chunk_count(half) if half % PIECE == 0 else 1
    size = half // pieces
    twice = doubler()
    totals = []
    for side in range(2):
        total = None
        for c in range(pieces):
            block = jnp.concatenate([part[:, c * size : (c + 1) * size] for part in parts], axis=0)
            left = spread(block, twice)
            start = side * half + c * size
            product = dot(left, up_ref.at[pl.ds(start, size)].reshape(2 * size, hidden_width)[...])
            total = product if total is None else total + product
        totals.append(total)
    height = count * lines
    slots = lines // 2

    def shifted(a, by):
        return pltpu.roll(a, by % a.shape[0], 0)

    top = lax.rem(iota((height, 1), 0), lines) < slots
    total = totals[0] + shifted(totals[1], -slots)
    hidden = gated(total)
    hidden = jnp.where(top, hidden, shifted(hidden, slots)).astype(BF16)
    for c in range(pieces):
        start = c * size
        first = dot(hidden, down_ref[:, start : start + size])
        second = dot(hidden, down_ref[:, half + start : half + start + size])
        scatter_rows(outs, slice(start, start + size), jnp.where(top, first, second))


def run_expert(parts, up, down):
    count = len(parts)
    sent = bundles(count, *parts[0].shape)
    vmem = pl.BlockSpec(memory_space=pltpu.VMEM)
    return pl.pallas_call(
        functools.partial(expert_kernel, count),
        out_shape=sent,
        in_specs=[vmem] * (count + 2),
        out_specs=[vmem] * len(sent),
        compiler_params=pltpu.CompilerParams(vmem_limit_bytes=16 * MIB),
        cost_estimate=pl.CostEstimate(flops=10**8, bytes_accessed=13 * 10**6, transcendentals=0),
        name="routed",
    )(*parts, up, down)


def seat_kernel(count, capacity, source_ref, *refs):
    parts, keep_ref, send_ref = refs[:count], refs[count], refs[count + 1]
    lines, half = parts[0].shape
    slots = lines // 2
    me = lax.axis_index("expert")
    side = lax.rem(lax.axis_index("replica"), 2)
    shape = (count * capacity, count * lines)
    seat, line = iota(shape, 0), iota(shape, 1)
    within = lax.rem(line, lines)
    slot = lax.rem(within, slots)
    expert = me ^ (line // lines)
    home = jnp.zeros(shape, I32)
    for index in range(count):
        home = jnp.where(expert == source_ref[index], index, home)
    target = jnp.where(slot < capacity, expert * capacity + slot, home * capacity + slot - capacity)
    here = (target == seat).astype(F32)
    second = (within >= slots).astype(I32)
    keep = jnp.where(second == side, here, 0.0).astype(BF16)
    send = jnp.where(second == side, 0.0, here).astype(BF16)
    pieces = chunk_count(half) if half % PIECE == 0 else 1
    size = half // pieces
    for c in range(pieces):
        cols = slice(c * size, (c + 1) * size)
        block = jnp.concatenate([part[:, cols] for part in parts], axis=0)
        keep_ref[:, cols] = dot(keep, block).astype(BF16)
        send_ref[:, cols] = dot(send, block).astype(BF16)


def seat_answers(parts, copy_source, capacity):
    count = len(parts)
    vmem = pl.BlockSpec(memory_space=pltpu.VMEM)
    shape = jax.ShapeDtypeStruct((count * capacity, parts[0].shape[1]), BF16)
    return pl.pallas_call(
        functools.partial(seat_kernel, count, capacity),
        out_shape=[shape, shape],
        in_specs=[pl.BlockSpec(memory_space=pltpu.SMEM)] + [vmem] * count,
        out_specs=[vmem, vmem],
        compiler_params=pltpu.CompilerParams(vmem_limit_bytes=16 * MIB),
        cost_estimate=pl.CostEstimate(flops=10**7, bytes_accessed=10**5, transcendentals=0),
        name="seats",
    )(copy_source, *parts)


def mix_kernel(near_ref, odd_ref, gate_ref, mine_ref, other_ref, out_ref):
    side = lax.rem(lax.axis_index("replica"), 2)
    seats, half = mine_ref.shape
    gates = gate_ref[:, :seats]
    high = gates.astype(BF16)
    left = gates - high.astype(F32)
    middle = left.astype(BF16)
    low = (left - middle.astype(F32)).astype(BF16)
    for position in range(2):
        cols = slice(position * half, (position + 1) * half)
        answers = jnp.where(side == position, mine_ref[...], other_ref[...])
        routed = dot(high, answers) + dot(middle, answers) + dot(low, answers)
        base = near_ref[:, cols] + odd_ref[:, cols].astype(F32)
        out_ref[:, cols] = (base + routed).astype(BF16)


def mix(near, odd, gates, mine, other):
    vmem = pl.BlockSpec(memory_space=pltpu.VMEM)
    return pl.pallas_call(
        mix_kernel,
        out_shape=jax.ShapeDtypeStruct(near.shape, BF16),
        in_specs=[vmem] * 5,
        out_specs=vmem,
        compiler_params=pltpu.CompilerParams(vmem_limit_bytes=16 * MIB),
        cost_estimate=pl.CostEstimate(flops=10**8, bytes_accessed=2 * 10**6, transcendentals=0),
        name="mix",
    )(near, odd, gates, mine, other)


def swap(array, axis, distance):
    pairs = [(i, i ^ distance) for i in range(lax.axis_size(axis))]
    return lax.ppermute(array, axis, pairs)


def exchange(blocks, axis):
    count = len(blocks)
    if count == 1:
        return blocks
    half = count // 2
    high = blocks[half] if half == 1 else jnp.concatenate(blocks[half:], axis=0)
    got = jnp.split(swap(high, axis, half), half, axis=0)
    return exchange(blocks[:half], axis) + exchange(got, axis)


def exchange_bundles(sent, axis, then):
    count = lax.axis_size(axis)
    half = count // 2
    if half == 0:
        return list(sent)
    got = swap(sent[half], axis, half)
    near, got = then(exchange(list(sent[:half]), axis), got)
    return near + exchange(jnp.split(got, half, axis=0), axis)


def add(a, b):
    return (a.astype(F32) + b.astype(F32)).astype(BF16)


def shards(
    tokens,
    route_ids,
    route_gates,
    copy_source,
    copy_share,
    w_gate_up,
    w_down,
    shared_gate_up,
    shared_down,
):
    experts = lax.axis_size("expert")
    replicas = lax.axis_size("replica")
    rows = tokens.shape[0]
    capacity = max(2, rows * 3 // 64)
    even, odd, table = line_plan(replicas)
    even_pairs = [(i, i ^ 1) for i in range(replicas)]
    odd_pairs = [(i, i + 1 if i % 2 else i - 1) for i in range(1, replicas - 1)]
    gates, tokens, head, *outgoing = plan(
        route_ids, route_gates, copy_source, copy_share, tokens, shared_gate_up, experts, capacity
    )
    parts = shared(tokens, head, shared_gate_up, shared_down, table)

    def after_shared(near, far):
        far, _ = lax.optimization_barrier((far, parts[-1]))
        return near, far

    incoming = exchange_bundles(outgoing, "expert", after_shared)
    sums = [None, None]

    def phase(number, *after):
        got_even, got_odd = sums
        if got_even is not None and after:
            got_even, *_ = lax.optimization_barrier((got_even, *after))
        if got_odd is not None:
            got_odd, _ = lax.optimization_barrier((got_odd, got_even[:8, :128]))
            got_even, got_odd = lax.optimization_barrier((got_even, got_odd))
        send_even, send_odd = parts[even[number]], None
        if number in odd:
            send_odd = add(parts[odd[number]], got_even)
        if got_odd is not None:
            send_even = add(send_even, got_odd)
        elif got_even is not None:
            send_even, got_even = lax.optimization_barrier((send_even, got_even))
        sums[0] = lax.ppermute(send_even, "replica", even_pairs)
        sums[1] = lax.ppermute(send_odd, "replica", odd_pairs) if number in odd else None
        return [send_even] if send_odd is None else [send_even, send_odd]

    phase(1)
    results = run_expert(incoming, w_gate_up[0], w_down[0])

    def after_first(near, far):
        if replicas > 2:
            far, *_ = lax.optimization_barrier((far, *phase(2, near[-1])))
        return near, far

    answers = exchange_bundles(results, "expert", after_first)
    keep, send = seat_answers(answers, copy_source, capacity)
    number, distance = 3, 2
    got, mine = swap(send, "replica", 1), keep
    while True:
        if number < replicas:
            got, *_ = lax.optimization_barrier((got, *phase(number)))
            number += 1
        mine = add(mine, got)
        if distance >= replicas:
            break
        got = swap(mine, "replica", distance)
        distance *= 2
    other = swap(mine, "replica", 1)
    for rest in range(number, replicas):
        phase(rest, mine)
    got_even, got_odd = sums
    share = rows // replicas
    own_gates = lax.dynamic_slice_in_dim(gates, lax.axis_index("replica") * share, share, 0)
    if got_odd is None:
        got_odd = jnp.zeros_like(got_even)
    near = parts[-1].astype(F32) + got_even.astype(F32)
    got_odd, near = lax.optimization_barrier((got_odd, near))
    return mix(near, got_odd, own_gates, mine, other)


def solution(mesh):
    return jax.shard_map(
        shards,
        mesh=mesh,
        in_specs=(
            P(("group", "expert"), None),
            P(("group", "expert"), None),
            P(("group", "expert"), None),
            P("group"),
            P("group"),
            P("expert", None, None, "replica"),
            P("expert", "replica", None),
            P(None, None, "replica"),
            P("replica", None),
        ),
        out_specs=P(("group", "expert", "replica"), None),
        check_vma=False,
    )
```

```python
import functools

import jax
import jax.numpy as jnp
from jax import lax
from jax.experimental import pallas as pl
from jax.experimental.pallas import tpu as pltpu
from jax.sharding import PartitionSpec as P

BF16 = jnp.bfloat16
F32 = jnp.float32
I32 = jnp.int32
PIECE = 256
MIB = 1 << 20


def iota(shape, dim):
    return lax.broadcasted_iota(I32, shape, dim)


def dot(a, b):
    return jnp.dot(a, b, preferred_element_type=F32)


def in_hbm(*arrays):
    return [pltpu.with_memory_space_constraint(array, pltpu.HBM) for array in arrays]


def chunk_count(width):
    for count in (4, 2, 1):
        if width % (count * PIECE) == 0:
            return count
    raise ValueError(width)


def scatter_rows(outs, columns, values):
    first = 0
    for out in outs:
        last = first + out.shape[0]
        out[:, columns] = values[first:last].astype(BF16)
        first = last


def bundles(experts, lines, width):
    half = max(1, experts // 2)
    heights = [lines] * half + [lines * (experts - half)] * (experts > half)
    return [pltpu.VMEM((height, width), BF16) for height in heights]


def plan_kernel(
    experts, capacity, share_hbm, source_hbm, ids_hbm, gates_hbm, tokens_hbm, up_hbm, gate_out, tokens_ref, head_ref, *rest
):
    *outs, share_ref, source_ref, ids_ref, gates_ref, sems = rest
    copies = [
        pltpu.make_async_copy(source, target, sems.at[number])
        for number, (source, target) in enumerate(
            [
                (ids_hbm, ids_ref),
                (share_hbm, share_ref),
                (source_hbm, source_ref),
                (gates_hbm, gates_ref),
                (tokens_hbm, tokens_ref),
                (up_hbm.at[pl.ds(0, head_ref.shape[0])], head_ref),
            ]
        )
    ]
    for copy in copies:
        copy.start()
    for copy in copies[:4]:
        copy.wait()
    ids = ids_ref[...]
    gates = gates_ref[...]
    top, rows = ids.shape
    me = lax.axis_index("expert")
    inside = ids < experts
    limit = jnp.zeros_like(ids)
    home = jnp.zeros_like(ids)
    for index in range(experts):
        limit = jnp.where(ids == index, share_ref[index], limit)
        home = jnp.where(ids == source_ref[index], index, home)
    by_copy = inside & (iota((top, rows), 1) < limit)
    holder = jnp.where(by_copy, home, ids)
    members = [jnp.where(inside & (holder == index), 1.0, 0.0) for index in range(experts)]
    earlier = jnp.where(iota((rows, rows), 0) < iota((rows, rows), 1), 1.0, 0.0).astype(BF16)
    rank = jnp.zeros((top, rows), F32)
    for index in range(experts):
        member = members[index]
        counts = jnp.broadcast_to(jnp.sum(member, axis=0, keepdims=True), (8, rows))
        running = dot(counts.astype(BF16), earlier)[:1]
        lines = []
        for k in range(top):
            lines.append(running)
            running = running + member[k : k + 1]
        rank = rank + member * jnp.concatenate(lines, axis=0)
    rank = rank.astype(I32)
    served = inside & (rank < capacity)
    slots = 2 * capacity
    place = jnp.where(served, ids * slots + rank + jnp.where(by_copy, capacity, 0), -1)
    seat = jnp.where(served, holder * capacity + rank, -1)
    seats = jnp.zeros((rows, rows), F32)
    for k in range(top):
        seats = seats + jnp.where(seat[k : k + 1] == iota((rows, rows), 0), gates[k : k + 1], 0.0)
    gate_out[...] = seats.T
    height = experts * 2 * slots
    line = iota((height, 1), 0)
    within = lax.rem(line, 2 * slots)
    wanted = (me ^ (line // (2 * slots))) * slots + lax.rem(within, slots)
    pick = jnp.zeros((height, rows), F32)
    for k in range(top):
        pick = pick + jnp.where(place[k : k + 1] == wanted, 1.0, 0.0)
    first = jnp.where(within < slots, pick, 0.0).astype(BF16)
    second = jnp.where(within < slots, 0.0, pick).astype(BF16)
    copies[4].wait()
    half = tokens_ref.shape[1] // 2
    step = half // chunk_count(half) if half % PIECE == 0 else half
    for start in range(0, half, step):
        picked = dot(first, tokens_ref[:, start : start + step]) + dot(
            second, tokens_ref[:, half + start : half + start + step]
        )
        scatter_rows(outs, slice(start, start + step), picked)
    copies[5].wait()


def plan(route_ids, route_gates, copy_source, copy_share, tokens, up, experts, capacity):
    rows, width = tokens.shape
    sent = bundles(experts, 4 * capacity, width // 2)
    vmem = pl.BlockSpec(memory_space=pltpu.VMEM)
    hbm = pl.BlockSpec(memory_space=pltpu.HBM)
    return pl.pallas_call(
        functools.partial(plan_kernel, experts, capacity),
        out_shape=[
            pltpu.VMEM((rows, rows), F32),
            pltpu.VMEM((rows, width), BF16),
            pltpu.VMEM((width // 2,) + up.shape[1:], BF16),
        ]
        + sent,
        in_specs=[hbm] * 6,
        out_specs=[vmem] * (len(sent) + 3),
        scratch_shapes=[
            pltpu.SMEM(copy_share.shape, I32),
            pltpu.SMEM(copy_source.shape, I32),
            pltpu.VMEM(route_ids.shape[::-1], I32),
            pltpu.VMEM(route_gates.shape[::-1], F32),
            pltpu.SemaphoreType.DMA((6,)),
        ],
        compiler_params=pltpu.CompilerParams(vmem_limit_bytes=16 * MIB),
        cost_estimate=pl.CostEstimate(flops=10**8, bytes_accessed=4 * 10**6, transcendentals=0),
        name="plan",
    )(*in_hbm(copy_share, copy_source, route_ids.T, route_gates.T, tokens, up))


def doubler():
    shape = (PIECE, 2 * PIECE)
    return jnp.where(iota(shape, 1) // 2 == iota(shape, 0), 1.0, 0.0).astype(BF16)


def spread(block, twice):
    parts = []
    for start in range(0, block.shape[1], PIECE):
        both = dot(block[:, start : start + PIECE], twice)
        even = lax.rem(iota(both.shape, 1), 2) == 0
        gate = jnp.where(even, both, 0.0).astype(BF16)
        up = jnp.where(even, 0.0, both).astype(BF16)
        parts.append(jnp.concatenate([gate, up], axis=0))
    return jnp.concatenate(parts, axis=1)


def gated(total):
    rows = total.shape[0] // 2
    gate = total[:rows]
    return gate / (1.0 + jnp.exp(-gate)) * total[rows:]


def line_plan(count):
    even, odd, table = {}, {}, []
    for phase in range(1, count):
        for parity, names in ((0, even), (1, odd)):
            need = {}
            for i in range(count):
                rises = i % 2 == parity
                other = i + 1 if rises else i - 1
                shard = count - phase + i if rises else i - count + phase
                if 0 <= other < count and (i <= phase - 1 if rises else i >= count - phase):
                    need[i] = shard
            if not need:
                continue
            for number, held in enumerate(table):
                if all(held.get(i, shard) == shard for i, shard in need.items()):
                    break
            else:
                number = len(table)
                table.append({})
            table[number].update(need)
            names[phase] = number
    table.append({i: i for i in range(count)})
    return even, odd, [[held.get(i, i) for i in range(count)] for held in table]


def shared_kernel(table, x_ref, head_ref, up_hbm, down_hbm, *rest):
    outs, rest = rest[: len(table)], rest[len(table) :]
    up_ref, down_ref, hidden_ref, up_sem, down_sem = rest
    rows, width = x_ref.shape
    share = outs[0].shape[0]
    hidden_width = up_ref.shape[2]
    count = chunk_count(width)
    size = width // count
    up_copies, down_copies = [], []
    known = head_ref.shape[0] // size
    for c in range(count - known):
        there, here = pl.ds((known + c) * size, size), pl.ds(c * size, size)
        up_copies.append(pltpu.make_async_copy(up_hbm.at[there], up_ref.at[here], up_sem.at[c]))
        up_copies[-1].start()
    for c in range(count):
        part = pl.ds(c * size, size)
        down_copies.append(
            pltpu.make_async_copy(down_hbm.at[:, part], down_ref.at[:, part], down_sem.at[c])
        )
        down_copies[-1].start()
    twice = doubler()
    total = None
    for c in range(count):
        left = spread(x_ref[:, c * size : (c + 1) * size], twice)
        source, place = head_ref, c
        if c >= known:
            source, place = up_ref, c - known
            up_copies[place].wait()
        weights = source.at[pl.ds(place * size, size)].reshape(2 * size, hidden_width)[...]
        product = dot(left, weights)
        total = product if total is None else total + product
    hidden_ref[...] = gated(total).astype(BF16)
    index = lax.axis_index("replica")
    picked = []
    for held in table:
        number = jnp.int32(0)
        for i, shard in enumerate(held):
            number = jnp.where(index == i, shard, number)
        picked.append(hidden_ref[pl.ds(pl.multiple_of(number * share, share), share), :])
    hidden = jnp.concatenate(picked, axis=0)
    for c in range(count):
        down_copies[c].wait()
        result = dot(hidden, down_ref[:, c * size : (c + 1) * size]).astype(BF16)
        for number, out in enumerate(outs):
            out[:, c * size : (c + 1) * size] = result[number * share : (number + 1) * share]


def shared(tokens, head, up, down, table):
    rows, width = tokens.shape
    count = chunk_count(width)
    share = rows // len(table[0])
    vmem = pl.BlockSpec(memory_space=pltpu.VMEM)
    return pl.pallas_call(
        functools.partial(shared_kernel, table),
        out_shape=[pltpu.VMEM((share, width), BF16)] * len(table),
        in_specs=[vmem] * 2 + [pl.BlockSpec(memory_space=pltpu.HBM)] * 2,
        out_specs=[vmem] * len(table),
        scratch_shapes=[
            pltpu.VMEM((width - head.shape[0],) + up.shape[1:], BF16),
            pltpu.VMEM(down.shape, BF16),
            pltpu.VMEM((rows, down.shape[0]), BF16),
            pltpu.SemaphoreType.DMA((count,)),
            pltpu.SemaphoreType.DMA((count,)),
        ],
        compiler_params=pltpu.CompilerParams(vmem_limit_bytes=18 * MIB),
        cost_estimate=pl.CostEstimate(flops=3 * 10**9, bytes_accessed=25 * 10**6, transcendentals=0),
        name="shared",
    )(tokens, head, *in_hbm(up, down))


def expert_kernel(count, *refs):
    parts, up_ref, down_ref, outs = refs[:count], refs[count], refs[count + 1], refs[count + 2 :]
    lines, half = parts[0].shape
    hidden_width = up_ref.shape[2]
    pieces = chunk_count(half) if half % PIECE == 0 else 1
    size = half // pieces
    twice = doubler()
    totals = []
    for side in range(2):
        total = None
        for c in range(pieces):
            block = jnp.concatenate([part[:, c * size : (c + 1) * size] for part in parts], axis=0)
            left = spread(block, twice)
            start = side * half + c * size
            product = dot(left, up_ref.at[pl.ds(start, size)].reshape(2 * size, hidden_width)[...])
            total = product if total is None else total + product
        totals.append(total)
    height = count * lines
    slots = lines // 2

    def shifted(a, by):
        return pltpu.roll(a, by % a.shape[0], 0)

    top = lax.rem(iota((height, 1), 0), lines) < slots
    total = totals[0] + shifted(totals[1], -slots)
    hidden = gated(total)
    hidden = jnp.where(top, hidden, shifted(hidden, slots)).astype(BF16)
    for c in range(pieces):
        start = c * size
        first = dot(hidden, down_ref[:, start : start + size])
        second = dot(hidden, down_ref[:, half + start : half + start + size])
        scatter_rows(outs, slice(start, start + size), jnp.where(top, first, second))


def run_expert(parts, up, down):
    count = len(parts)
    sent = bundles(count, *parts[0].shape)
    vmem = pl.BlockSpec(memory_space=pltpu.VMEM)
    return pl.pallas_call(
        functools.partial(expert_kernel, count),
        out_shape=sent,
        in_specs=[vmem] * (count + 2),
        out_specs=[vmem] * len(sent),
        compiler_params=pltpu.CompilerParams(vmem_limit_bytes=16 * MIB),
        cost_estimate=pl.CostEstimate(flops=10**8, bytes_accessed=13 * 10**6, transcendentals=0),
        name="routed",
    )(*parts, up, down)


def seat_kernel(count, capacity, source_ref, *refs):
    parts, keep_ref, send_ref = refs[:count], refs[count], refs[count + 1]
    lines, half = parts[0].shape
    slots = lines // 2
    me = lax.axis_index("expert")
    side = lax.rem(lax.axis_index("replica"), 2)
    shape = (count * capacity, count * lines)
    seat, line = iota(shape, 0), iota(shape, 1)
    within = lax.rem(line, lines)
    slot = lax.rem(within, slots)
    expert = me ^ (line // lines)
    home = jnp.zeros(shape, I32)
    for index in range(count):
        home = jnp.where(expert == source_ref[index], index, home)
    target = jnp.where(slot < capacity, expert * capacity + slot, home * capacity + slot - capacity)
    here = (target == seat).astype(F32)
    second = (within >= slots).astype(I32)
    keep = jnp.where(second == side, here, 0.0).astype(BF16)
    send = jnp.where(second == side, 0.0, here).astype(BF16)
    pieces = chunk_count(half) if half % PIECE == 0 else 1
    size = half // pieces
    for c in range(pieces):
        cols = slice(c * size, (c + 1) * size)
        block = jnp.concatenate([part[:, cols] for part in parts], axis=0)
        keep_ref[:, cols] = dot(keep, block).astype(BF16)
        send_ref[:, cols] = dot(send, block).astype(BF16)


def seat_answers(parts, copy_source, capacity):
    count = len(parts)
    vmem = pl.BlockSpec(memory_space=pltpu.VMEM)
    shape = jax.ShapeDtypeStruct((count * capacity, parts[0].shape[1]), BF16)
    return pl.pallas_call(
        functools.partial(seat_kernel, count, capacity),
        out_shape=[shape, shape],
        in_specs=[pl.BlockSpec(memory_space=pltpu.SMEM)] + [vmem] * count,
        out_specs=[vmem, vmem],
        compiler_params=pltpu.CompilerParams(vmem_limit_bytes=16 * MIB),
        cost_estimate=pl.CostEstimate(flops=10**7, bytes_accessed=10**5, transcendentals=0),
        name="seats",
    )(copy_source, *parts)


def mix_kernel(near_ref, odd_ref, gate_ref, mine_ref, other_ref, out_ref):
    side = lax.rem(lax.axis_index("replica"), 2)
    seats, half = mine_ref.shape
    gates = gate_ref[:, :seats]
    high = gates.astype(BF16)
    left = gates - high.astype(F32)
    middle = left.astype(BF16)
    low = (left - middle.astype(F32)).astype(BF16)
    for position in range(2):
        cols = slice(position * half, (position + 1) * half)
        answers = jnp.where(side == position, mine_ref[...], other_ref[...])
        routed = dot(high, answers) + dot(middle, answers) + dot(low, answers)
        base = near_ref[:, cols] + odd_ref[:, cols].astype(F32)
        out_ref[:, cols] = (base + routed).astype(BF16)


def mix(near, odd, gates, mine, other):
    vmem = pl.BlockSpec(memory_space=pltpu.VMEM)
    return pl.pallas_call(
        mix_kernel,
        out_shape=jax.ShapeDtypeStruct(near.shape, BF16),
        in_specs=[vmem] * 5,
        out_specs=vmem,
        compiler_params=pltpu.CompilerParams(vmem_limit_bytes=16 * MIB),
        cost_estimate=pl.CostEstimate(flops=10**8, bytes_accessed=2 * 10**6, transcendentals=0),
        name="mix",
    )(near, odd, gates, mine, other)


def swap(array, axis, distance):
    pairs = [(i, i ^ distance) for i in range(lax.axis_size(axis))]
    return lax.ppermute(array, axis, pairs)


def exchange(blocks, axis):
    count = len(blocks)
    if count == 1:
        return blocks
    half = count // 2
    high = blocks[half] if half == 1 else jnp.concatenate(blocks[half:], axis=0)
    got = jnp.split(swap(high, axis, half), half, axis=0)
    return exchange(blocks[:half], axis) + exchange(got, axis)


def exchange_bundles(sent, axis, then):
    count = lax.axis_size(axis)
    half = count // 2
    if half == 0:
        return list(sent)
    got = swap(sent[half], axis, half)
    near, got = then(exchange(list(sent[:half]), axis), got)
    return near + exchange(jnp.split(got, half, axis=0), axis)


def add(a, b):
    return (a.astype(F32) + b.astype(F32)).astype(BF16)


def shards(
    tokens,
    route_ids,
    route_gates,
    copy_source,
    copy_share,
    w_gate_up,
    w_down,
    shared_gate_up,
    shared_down,
):
    experts = lax.axis_size("expert")
    replicas = lax.axis_size("replica")
    rows = tokens.shape[0]
    capacity = max(2, rows * 3 // 64)
    even, odd, table = line_plan(replicas)
    even_pairs = [(i, i ^ 1) for i in range(replicas)]
    odd_pairs = [(i, i + 1 if i % 2 else i - 1) for i in range(1, replicas - 1)]
    gates, tokens, head, *outgoing = plan(
        route_ids, route_gates, copy_source, copy_share, tokens, shared_gate_up, experts, capacity
    )
    parts = shared(tokens, head, shared_gate_up, shared_down, table)

    def after_shared(near, far):
        far, _ = lax.optimization_barrier((far, parts[-1]))
        return near, far

    incoming = exchange_bundles(outgoing, "expert", after_shared)
    sums = [None, None]

    def phase(number, *after):
        got_even, got_odd = sums
        if got_even is not None and after:
            got_even, *_ = lax.optimization_barrier((got_even, *after))
        if got_odd is not None:
            held = parts[odd[number]]
            cut = held.shape[1] // 8
            left = add(held[:, :cut], got_even[:, :cut])
            got_odd, left = lax.optimization_barrier((got_odd, left))
            got_even, got_odd = lax.optimization_barrier((got_even, got_odd))
        send_even, send_odd = parts[even[number]], None
        if number in odd:
            send_odd = add(parts[odd[number]], got_even)
        if got_odd is not None:
            send_odd = jnp.concatenate([left, add(held[:, cut:], got_even[:, cut:])], axis=1)
            send_even = add(send_even, got_odd)
        elif got_even is not None:
            send_even, got_even = lax.optimization_barrier((send_even, got_even))
        sums[0] = lax.ppermute(send_even, "replica", even_pairs)
        sums[1] = lax.ppermute(send_odd, "replica", odd_pairs) if number in odd else None
        return [send_even] if send_odd is None else [send_even, send_odd]

    phase(1)
    results = run_expert(incoming, w_gate_up[0], w_down[0])

    def after_first(near, far):
        if replicas > 2:
            far, *_ = lax.optimization_barrier((far, *phase(2, near[-1])))
        return near, far

    answers = exchange_bundles(results, "expert", after_first)
    keep, send = seat_answers(answers, copy_source, capacity)
    number, distance = 3, 2
    got, mine = swap(send, "replica", 1), keep
    while True:
        if number < replicas:
            got, *_ = lax.optimization_barrier((got, *phase(number)))
            number += 1
        mine = add(mine, got)
        if distance >= replicas:
            break
        got = swap(mine, "replica", distance)
        distance *= 2
    other = swap(mine, "replica", 1)
    for rest in range(number, replicas):
        phase(rest, mine)
    got_even, got_odd = sums
    share = rows // replicas
    own_gates = lax.dynamic_slice_in_dim(gates, lax.axis_index("replica") * share, share, 0)
    if got_odd is None:
        got_odd = jnp.zeros_like(got_even)
    near = parts[-1].astype(F32) + got_even.astype(F32)
    got_odd, near = lax.optimization_barrier((got_odd, near))
    return mix(near, got_odd, own_gates, mine, other)


def solution(mesh):
    return jax.shard_map(
        shards,
        mesh=mesh,
        in_specs=(
            P(("group", "expert"), None),
            P(("group", "expert"), None),
            P(("group", "expert"), None),
            P("group"),
            P("group"),
            P("expert", None, None, "replica"),
            P("expert", "replica", None),
            P(None, None, "replica"),
            P("replica", None),
        ),
        out_specs=P(("group", "expert", "replica"), None),
        check_vma=False,
    )
```
